512 devices in a mesh: row: 16 (over x, z_lo), col: 32 (over y, z_hi, core).
Axes of the slice: x: 4, y: 4, z: 16 (z_hi: 4, z_lo: 4; z = z_hi * 4 + z_lo), core: 2. Of those that a mesh axis runs over, the one named last changes fastest.
Arguments:
- queries: bfloat16 [16, 32, 128, 512], P(None, 'col', 'row'), may hold values from -6 to 6
- grad_output: bfloat16 [16, 32, 128, 512], P(None, 'col', 'row'), may hold values from -60 to 60
- attn_output: bfloat16 [16, 32, 128, 512], P(None, 'col', 'row'), may hold values from -1.796875 to 1.796875
- key_states: bfloat16 [65536, 128], P(('row', 'col')), may hold values from -6 to 6
- value_states: bfloat16 [65536, 128], P(('row', 'col')), may hold values from -6 to 6
- log_sum: float32 [16, 32, 128, 4], P(None, 'col', 'row'), may hold values from -1 to 12
- segment: int32 [65536], replicated, may hold values from 0 to 10, as said below
- prefix: int32 [65536], replicated, may hold values from 0 to 10, as said below
- block_list: int32 [16, 32, 16, 32], P(None, 'col', 'row'), may hold values from 0 to 31, as said below
- block_count: int32 [16, 32, 16], P(None, 'col', 'row'), may hold values from 0 to 32
Outputs:
- grad_query: bfloat16 [16, 32, 128, 512], P(None, 'col', 'row')
- grad_key: bfloat16 [65536, 128], P(('row', 'col'))
- grad_value: bfloat16 [65536, 128], P(('row', 'col'))
The draws below stay inside these ranges and needn't reach their ends.
Inputs may be any that keep to these rules, and one draw needn't show every extreme that they name: Non-decreasing along the pack, each segment a nonempty run of positions; segment 0 is a prompt that covers the first 8192 positions and segment 1 is a response to it. `prefix`: segment[p] itself for a position of a prompt; for a position of a response, the id of an earlier prompt segment, the same for the whole response. `block_list`: for query block (j, c) and key group g, the key blocks of the group (numbered within it) that hold a key allowed to some query of the block by the segment and causal rules, ascending in the first block_count[j, c, g] entries; the other entries are 0.
All inputs are finite; a program needn't handle non-finite values.
Results may differ from the reference program's by a relative error of at most 0.015.
Values may be sent and summed in bfloat16 or wider, within the bound.
No kernel may reach another device: no remote copies, remote signals or barrier semaphores. Data moves between devices by JAX's collectives and lax.ppermute only.
A program may use at most 64 MiB of HBM per device.

```python
import jax
import jax.numpy as jnp
from jax import lax

TOK_DEV = 128
HEADS = 4
HDIM = 128
BLK = 128
TOKENS = 65536
QBLOCKS = 16
KBLOCKS = 32
NBLOCKS = 512
N_ROW = 16
N_COL = 32


def pack_layout(key):
    opening = 2 * TOK_DEV * N_COL
    spread = jax.random.permutation(jax.random.fold_in(key, 11), TOKENS - opening - 1)[:9]
    cut_points = jnp.sort(spread.astype(jnp.int32) + opening + 1)
    starts = jnp.concatenate([jnp.zeros((1,), jnp.int32), jnp.full((1,), opening, jnp.int32), cut_points])
    finish = jnp.concatenate([starts[1:], jnp.full((1,), TOKENS, jnp.int32)])
    lengths = finish - starts
    places = jnp.arange(TOKENS, dtype=jnp.int32)
    segment = jnp.sum((places[:, None] >= starts[None, 1:]).astype(jnp.int32), axis=1)
    labels = jnp.arange(11, dtype=jnp.int32)
    dice_roll = jax.random.randint(jax.random.fold_in(key, 12), (11,), 0, 4)
    prompt_flags = ((dice_roll == 0) | (labels == 0) | (labels == 10)) & (labels != 1)
    owners = lax.cummax(jnp.where(prompt_flags, labels, 0), axis=0)
    prefix = owners[segment]
    visible = places - starts[segment] + 1 + jnp.where(prefix != segment, lengths[prefix], 0)
    return (segment, prefix, visible, owners)


def block_tables(key):
    segment, prefix, visible, owners = pack_layout(key)
    labels = jnp.arange(11, dtype=jnp.int32)
    grouped = segment.reshape(NBLOCKS, BLK)
    lowest = grouped[:, 0]
    highest = grouped[:, BLK - 1]
    holding = ((labels[None, :] >= lowest[:, None]) & (labels[None, :] <= highest[:, None])).astype(jnp.int32)
    seeing = ((labels[:, None] == labels[None, :]) | (owners[:, None] == labels[None, :])).astype(jnp.int32)
    reached = jnp.dot(jnp.dot(holding, seeing), holding.T)
    blocks = jnp.arange(NBLOCKS, dtype=jnp.int32)
    active = (reached > 0) & (blocks[None, :] <= blocks[:, None])
    active = active.reshape(NBLOCKS, N_ROW, KBLOCKS)
    local_idx = jnp.arange(KBLOCKS, dtype=jnp.int32)
    ranked = jnp.argsort(jnp.where(active, local_idx, KBLOCKS + local_idx), axis=2).astype(jnp.int32)
    counted = jnp.sum(active.astype(jnp.int32), axis=2)
    listed = jnp.where(local_idx[None, None, :] < counted[:, :, None], ranked, 0)
    return (listed.reshape(QBLOCKS, N_COL, N_ROW, KBLOCKS), counted.reshape(QBLOCKS, N_COL, N_ROW))


def draw_segment(key, part):
    shared = pack_layout(key)
    return shared[0]


def draw_prefix(key, part):
    shared = pack_layout(key)
    return shared[1]


def draw_block_list(key, part):
    tables = block_tables(key)
    return tables[0]


def draw_block_count(key, part):
    tables = block_tables(key)
    return tables[1]


def draw_log_sum(key, part):
    shared = pack_layout(key)
    key = jax.random.fold_in(key, 4)
    baseline = jnp.log(shared[2].astype(jnp.float32)) + 0.5
    jitter = jax.random.uniform(key, (TOKENS, HEADS), jnp.float32, -0.3, 0.3)
    return (baseline[:, None] + jitter).reshape(QBLOCKS, N_COL, BLK, HEADS)


def block_scale(stream_key, extent, pieces, least, high):
    def one(dim, parts):
        steps = jax.random.uniform(jax.random.fold_in(jax.random.fold_in(stream_key, 6), dim), (parts,), jnp.float32, least / len(pieces), high / len(pieces))
        return jnp.repeat(jnp.exp(steps), extent[dim] // parts).reshape((-1,) + (1,) * (len(extent) - dim - 1))

    loudness = one(*pieces[0])
    for cut in pieces[1:]:
        loudness = loudness * one(*cut)
    return loudness


def scatter_about(rng, dims, scale, most, cuts=(), kind=jnp.bfloat16):
    values = scale * jax.random.normal(rng, dims, jnp.float32)
    if cuts:
        values = values * block_scale(rng, dims, cuts, -0.22, 0.18)
    return jnp.clip(values, -most, most).astype(kind)


def setup_inputs(seed: int = 0) -> dict:
    key_of = jax.random.split(jax.random.key(seed), 11)
    return {
        "queries": scatter_about(key_of[0], (QBLOCKS, N_COL, BLK, HEADS * HDIM), 1.0, 6.0, ((1, 32), (2, 16))),
        "grad_output": scatter_about(key_of[1], (QBLOCKS, N_COL, BLK, HEADS * HDIM), 10.0, 60.0, ((1, 32), (2, 16))),
        "attn_output": scatter_about(key_of[2], (QBLOCKS, N_COL, BLK, HEADS * HDIM), 0.3, 1.796875, ((1, 32), (2, 16))),
        "key_states": scatter_about(key_of[3], (TOKENS, HDIM), 1.0, 6.0, ((0, 512),)),
        "value_states": scatter_about(key_of[4], (TOKENS, HDIM), 1.0, 6.0, ((0, 512),)),
        "log_sum": draw_log_sum(jax.random.fold_in(key_of[10], 71), 0),
        "segment": draw_segment(jax.random.fold_in(key_of[10], 71), 0),
        "prefix": draw_prefix(jax.random.fold_in(key_of[10], 71), 0),
        "block_list": draw_block_list(jax.random.fold_in(key_of[10], 71), 0),
        "block_count": draw_block_count(jax.random.fold_in(key_of[10], 71), 0),
    }


def tile_terms(q_rows, do_rows, lse_rows, delta_rows, q_places, q_seg, q_pre, key_rows, value_rows, k_places, k_seg):
    scaling = HDIM ** -0.5
    allowed = (k_places[None, :] <= q_places[:, None]) & ((k_seg[None, :] == q_seg[:, None]) | (k_seg[None, :] == q_pre[:, None]))
    scores = jnp.einsum("nhd,kd->nhk", q_rows, key_rows) * scaling
    weights = jnp.where(allowed[:, None, :], jnp.exp(scores - lse_rows[:, :, None]), jnp.float32(0.0))
    weight_grad = jnp.einsum("nhd,kd->nhk", do_rows, value_rows)
    score_grad = weights * (weight_grad - delta_rows[:, :, None])
    weights_b = lax.optimization_barrier(weights.astype(jnp.bfloat16)).astype(jnp.float32)
    score_grad_b = lax.optimization_barrier(score_grad.astype(jnp.bfloat16)).astype(jnp.float32)
    query_new = jnp.einsum("nhk,kd->nhd", score_grad_b, key_rows) * scaling
    key_new = jnp.einsum("nhk,nhd->kd", score_grad_b, q_rows) * scaling
    value_new = jnp.einsum("nhk,nhd->kd", weights_b, do_rows)
    return query_new, key_new, value_new


def reference(queries, grad_output, attn_output, key_states, value_states, log_sum, segment, prefix, block_list, block_count):
    delta = jnp.sum((grad_output.astype(jnp.float32) * attn_output.astype(jnp.float32)).reshape(QBLOCKS, N_COL, BLK, HEADS, HDIM), axis=4)
    key_blocks = key_states.reshape(NBLOCKS, BLK, HDIM)
    value_blocks = value_states.reshape(NBLOCKS, BLK, HDIM)
    offsets = jnp.arange(BLK, dtype=jnp.int32)
    zero_rows = jnp.zeros((BLK, HEADS, HDIM), jnp.float32)
    zero_keys = jnp.zeros((TOKENS, HDIM), jnp.float32)

    def column(totals, col_at):
        def query_block(block_at, carried):
            block_at = jnp.asarray(block_at).astype(jnp.int32)
            query_out, key_part, value_part = carried
            q_rows = queries[block_at, col_at].reshape(BLK, HEADS, HDIM).astype(jnp.float32)
            do_rows = grad_output[block_at, col_at].reshape(BLK, HEADS, HDIM).astype(jnp.float32)
            lse_rows = log_sum[block_at, col_at]
            delta_rows = delta[block_at, col_at]
            q_places = ((block_at * N_COL + col_at) * BLK).astype(jnp.int32) + offsets
            q_seg = segment[q_places]
            q_pre = prefix[q_places]

            def key_group(group_at, running):
                group_at = jnp.asarray(group_at).astype(jnp.int32)
                query_sum, key_part, value_part = running

                def key_block(slot_at, inner):
                    slot_at = jnp.asarray(slot_at).astype(jnp.int32)
                    query_acc, key_part, value_part = inner
                    chosen = (group_at * KBLOCKS + block_list[block_at, col_at, group_at, slot_at]).astype(jnp.int32)
                    k_places = chosen * BLK + offsets
                    key_rows = lax.dynamic_index_in_dim(key_blocks, chosen, 0, keepdims=False).astype(jnp.float32)
                    value_rows = lax.dynamic_index_in_dim(value_blocks, chosen, 0, keepdims=False).astype(jnp.float32)
                    query_new, key_new, value_new = tile_terms(q_rows, do_rows, lse_rows, delta_rows, q_places, q_seg, q_pre, key_rows, value_rows, k_places, segment[k_places])
                    begin = (chosen * BLK).astype(jnp.int32)
                    key_part = lax.dynamic_update_slice_in_dim(key_part, lax.dynamic_slice_in_dim(key_part, begin, BLK, 0) + key_new, begin, 0)
                    value_part = lax.dynamic_update_slice_in_dim(value_part, lax.dynamic_slice_in_dim(value_part, begin, BLK, 0) + value_new, begin, 0)
                    return query_acc + query_new, key_part, value_part

                query_acc, key_part, value_part = lax.fori_loop(jnp.int32(0), block_count[block_at, col_at, group_at], key_block, (zero_rows, key_part, value_part))
                rounded = lax.optimization_barrier(query_acc.astype(jnp.bfloat16)).astype(jnp.float32)
                return query_sum + rounded, key_part, value_part

            query_sum, key_part, value_part = lax.fori_loop(0, N_ROW, key_group, (zero_rows, key_part, value_part))
            query_out = lax.dynamic_update_index_in_dim(query_out, query_sum.astype(jnp.bfloat16).reshape(BLK, HEADS * HDIM), block_at, 0)
            return query_out, key_part, value_part

        starting = (jnp.zeros((QBLOCKS, BLK, HEADS * HDIM), jnp.bfloat16), zero_keys, zero_keys)
        query_out, key_part, value_part = lax.fori_loop(0, QBLOCKS, query_block, starting)
        key_total, value_total = totals
        key_total = key_total + lax.optimization_barrier(key_part.astype(jnp.bfloat16)).astype(jnp.float32)
        value_total = value_total + lax.optimization_barrier(value_part.astype(jnp.bfloat16)).astype(jnp.float32)
        return (key_total, value_total), query_out

    (key_total, value_total), query_cols = lax.scan(column, (zero_keys, zero_keys), jnp.arange(N_COL, dtype=jnp.int32))
    grad_query = jnp.transpose(query_cols, (1, 0, 2, 3))
    return grad_query, key_total.astype(jnp.bfloat16), value_total.astype(jnp.bfloat16)
```

```python
import functools

import jax
import jax.numpy as jnp
from jax import lax
from jax.experimental import pallas as pl
from jax.experimental.pallas import tpu as pltpu
from jax.sharding import PartitionSpec as P

NX, NZL, NY, NZH, NCORE = 4, 4, 4, 4, 2
SEGMENTS = 11
LOG2E = 1.4426950408889634
NEVER = -(1 << 30)


def row_perm(dx, dzl):
    return [
        (x * NZL + z, ((x + dx) % NX) * NZL + (z + dzl) % NZL)
        for x in range(NX)
        for z in range(NZL)
    ]


def col_perm(dy, dzh, dcore):
    return [
        (
            (y * NZH + z) * NCORE + k,
            (((y + dy) % NY) * NZH + (z + dzh) % NZH) * NCORE + (k + dcore) % NCORE,
        )
        for y in range(NY)
        for z in range(NZH)
        for k in range(NCORE)
    ]


def split3(value):
    high = lax.reduce_precision(value, 8, 7)
    rest = value - high
    mid = lax.reduce_precision(rest, 8, 7)
    low = rest - mid
    return [part.astype(jnp.bfloat16) for part in (high, mid, low)]


def segment_table(segment, prefix):
    ids = jnp.arange(SEGMENTS, dtype=jnp.int32)
    start = jnp.sum((segment[None, :] < ids[:, None]).astype(jnp.int32), axis=1)
    finish = jnp.sum((segment[None, :] <= ids[:, None]).astype(jnp.int32), axis=1)
    owner = jnp.max(jnp.where(segment[None, :] == ids[:, None], prefix[None, :], 0), axis=1)
    picked = owner[:, None] == ids[None, :]
    low = jnp.sum(jnp.where(picked, start[None, :], 0), axis=1)
    high = jnp.sum(jnp.where(picked, finish[None, :], 0), axis=1)
    return jnp.stack([start, low, high])


def attention_kernel(
    jcount,
    ids_ref,
    table_ref,
    list_ref,
    count_ref,
    pay0,
    pay1,
    pay2,
    pay3,
    kv0,
    kv1,
    dq0,
    dq1,
    dq2,
    dq3,
    dkv_ref,
    k_scr,
    v_scr,
    kt_scr,
    dk_scr,
    dv_scr,
    lse_scr,
    delta_scr,
    q_scr,
    do_scr,
    qt_scr,
    dot_scr,
    dqt_scr,
):
    f32, bf16 = jnp.float32, jnp.bfloat16
    pays = (pay0, pay1, pay2, pay3)
    dqs = (dq0, dq1, dq2, dq3)
    rows = jcount * 32
    scale = 128.0 ** -0.5
    my_x, my_zl, my_c = ids_ref[0], ids_ref[1], ids_ref[2]
    my_y, my_zh, my_core, my_g = ids_ref[3], ids_ref[4], ids_ref[5], ids_ref[6]

    dk_scr[...] = jnp.zeros_like(dk_scr)
    dv_scr[...] = jnp.zeros_like(dv_scr)

    def prepare(slot, _):
        for half, ref in enumerate((kv0, kv1)):
            key = ref[slot, 0]
            k_scr[half * 16 + slot] = key
            v_scr[half * 16 + slot] = ref[slot, 1]
            kt_scr[half * 16 + slot] = key.T
        return 0

    lax.fori_loop(0, 16, prepare, 0)

    for xs in range(NX):
        terms = [
            pays[xs][pl.ds(8 * rows + part * 16, 16), :].astype(f32) for part in range(6)
        ]
        lanes = pl.ds(xs * 128, 128)
        lse_scr[:, lanes] = (terms[0] + terms[1] + terms[2]) * LOG2E
        delta_scr[:, lanes] = terms[3] + terms[4] + terms[5]

    lane = lax.broadcasted_iota(jnp.int32, (1, 512), 1)
    row_of = ((my_x + (lane >> 7)) & 3) * 4 + ((my_zl + (lane >> 5)) & 3)
    row_off = row_of * 8 + (lane & 7)
    key_iota = lax.broadcasted_iota(jnp.int32, (128, 512), 0)

    def query_block(j, _):
        count = count_ref[j]
        base = (j * 32 + my_c) * 128

        @pl.when(count == 0)
        def _():
            for xs in range(NX):
                for zs in range(NZL):
                    dqs[xs][pl.ds(zs * rows + j * 32, 32), :] = jnp.zeros((32, 128), bf16)

        @pl.when(count > 0)
        def _():
            for xs in range(NX):
                for zs in range(NZL):
                    at = (xs * NZL + zs) * 32
                    q_scr[pl.ds(at, 32), :] = pays[xs][pl.ds(zs * rows + j * 32, 32), :]
                    do_scr[pl.ds(at, 32), :] = pays[xs][
                        pl.ds((NZL + zs) * rows + j * 32, 32), :
                    ]
            qt_scr[...] = q_scr[...].T
            dot_scr[...] = do_scr[...].T
            dqt_scr[...] = jnp.zeros_like(dqt_scr)

            place = base + row_off
            own_low = jnp.zeros_like(place)
            pre_low = jnp.zeros_like(place)
            pre_high = jnp.zeros_like(place)
            first_low, last_low = jnp.int32(0), jnp.int32(0)
            tile_low, tile_high = jnp.int32(0), jnp.int32(0)
            for s in range(SEGMENTS):
                start, low, high = table_ref[0, s], table_ref[1, s], table_ref[2, s]
                here = place >= start
                own_low = jnp.where(here, start, own_low)
                pre_low = jnp.where(here, low, pre_low)
                pre_high = jnp.where(here, high, pre_high)
                first_low = jnp.where(base >= start, start, first_low)
                tile_low = jnp.where(base >= start, low, tile_low)
                tile_high = jnp.where(base >= start, high, tile_high)
                last_low = jnp.where(base + 127 >= start, start, last_low)
            pre_high = jnp.minimum(pre_high, place + 1)
            single = first_low == last_low
            tile_high = jnp.where(single, jnp.minimum(tile_high, base + 1), 0)
            lse_row = lse_scr[pl.ds(j, 1), :]
            delta_row = delta_scr[pl.ds(j, 1), :]

            def one(m, masked):
                slots, firsts = [], []
                for u in range(2):
                    at = 2 * m + u
                    key_id = list_ref[j, jnp.minimum(at, 31)]
                    slot = (
                        ((key_id & 1) ^ my_core) * 16
                        + (((key_id >> 3) - my_y) & 3) * 4
                        + (((key_id >> 1) - my_zh) & 3)
                    )
                    slots.append(slot)
                    firsts.append(jnp.where(at < count, (my_g * 32 + key_id) * 128, NEVER))
                pbs, dsbs = [], []
                for u in range(2):
                    scores = jnp.dot(
                        k_scr[slots[u]], qt_scr[...], preferred_element_type=f32
                    )
                    weights = jnp.exp2(scores * (scale * LOG2E) - lse_row)
                    if masked:
                        key_at = key_iota + firsts[u]
                        allowed = ((key_at >= own_low) & (key_at <= place)) | (
                            (key_at >= pre_low) & (key_at < pre_high)
                        )
                        weights = jnp.where(allowed, weights, 0.0)
                    weight_grad = jnp.dot(
                        v_scr[slots[u]], dot_scr[...], preferred_element_type=f32
                    )
                    score_grad = weights * (weight_grad - delta_row)
                    pb = weights.astype(bf16)
                    dsb = score_grad.astype(bf16)
                    dv_scr[slots[u]] += jnp.dot(pb, do_scr[...], preferred_element_type=f32)
                    dk_scr[slots[u]] += jnp.dot(dsb, q_scr[...], preferred_element_type=f32)
                    dsbs.append(dsb)
                keys_t = jnp.concatenate([kt_scr[slots[0]], kt_scr[slots[1]]], axis=1)
                dqt_scr[...] += jnp.dot(
                    keys_t, jnp.concatenate(dsbs, axis=0), preferred_element_type=f32
                )

            def step(m, _):
                full = 2 * m + 1 < count
                for u in range(2):
                    key_id = list_ref[j, jnp.minimum(2 * m + u, 31)]
                    first = (my_g * 32 + key_id) * 128
                    own = (first >= last_low) & (first + 127 <= base)
                    pre = (first >= tile_low) & (first + 128 <= tile_high)
                    full = full & (own | pre)

                @pl.when(full)
                def _():
                    one(m, False)

                @pl.when(jnp.logical_not(full))
                def _():
                    one(m, True)

                return 0

            lax.fori_loop(0, (count + 1) // 2, step, 0)
            dq = (dqt_scr[...] * scale).astype(bf16).T
            for xs in range(NX):
                for zs in range(NZL):
                    at = (xs * NZL + zs) * 32
                    dqs[xs][pl.ds(zs * rows + j * 32, 32), :] = dq[at : at + 32]

        return 0

    lax.fori_loop(0, jcount, query_block, 0)

    def finish(slot, _):
        for half in range(2):
            dkv_ref[half, slot, 0] = (dk_scr[half * 16 + slot] * scale).astype(bf16)
            dkv_ref[half, slot, 1] = dv_scr[half * 16 + slot].astype(bf16)
        return 0

    lax.fori_loop(0, 16, finish, 0)


def run_attention(ids, table, lists, counts, pays, kv0, kv1, jcount):
    f32, bf16 = jnp.float32, jnp.bfloat16
    rows = jcount * 32
    smem = pl.BlockSpec(memory_space=pltpu.SMEM)
    vmem = pl.BlockSpec(memory_space=pltpu.VMEM)
    part = jax.ShapeDtypeStruct((NZL * rows, 128), bf16)
    return pl.pallas_call(
        functools.partial(attention_kernel, jcount),
        out_shape=[part] * 4 + [jax.ShapeDtypeStruct((2, 16, 2, 128, 128), bf16)],
        in_specs=[smem] * 4 + [vmem] * 6,
        out_specs=[vmem] * 5,
        scratch_shapes=[
            pltpu.VMEM((32, 128, 128), bf16),
            pltpu.VMEM((32, 128, 128), bf16),
            pltpu.VMEM((32, 128, 128), bf16),
            pltpu.VMEM((32, 128, 128), f32),
            pltpu.VMEM((32, 128, 128), f32),
            pltpu.VMEM((16, 512), f32),
            pltpu.VMEM((16, 512), f32),
            pltpu.VMEM((512, 128), bf16),
            pltpu.VMEM((512, 128), bf16),
            pltpu.VMEM((128, 512), bf16),
            pltpu.VMEM((128, 512), bf16),
            pltpu.VMEM((128, 512), f32),
        ],
        compiler_params=pltpu.CompilerParams(vmem_limit_bytes=48 * 1024 * 1024),
        name="attention_backward",
    )(ids, table, lists, counts, *pays, kv0, kv1)


def total(parts):
    out = parts[0].astype(jnp.float32)
    for part in parts[1:]:
        out = out + part.astype(jnp.float32)
    return out.astype(jnp.bfloat16)


def on_device(
    queries,
    grad_output,
    attn_output,
    key_states,
    value_states,
    log_sum,
    segment,
    prefix,
    block_list,
    block_count,
):
    jcount = queries.shape[0]
    rows = jcount * 32
    row = lax.axis_index("row")
    col = lax.axis_index("col")
    my_x, my_zl = row // NZL, row % NZL
    my_y, my_zh, my_core = col // (NZH * NCORE), (col // NCORE) % NZH, col % NCORE
    ids = jnp.stack([my_x, my_zl, col, my_y, my_zh, my_core, row]).astype(jnp.int32)

    def heads_first(value):
        return value.reshape(jcount, 8, 4, 128).transpose(0, 2, 1, 3).reshape(rows, 128)

    with jax.named_scope("pack"):
        delta = jnp.sum(
            (grad_output.astype(jnp.float32) * attn_output.astype(jnp.float32)).reshape(
                jcount, 8, 4, 128
            ),
            axis=3,
        )
        lse = log_sum.reshape(jcount, 8, 4)
        aux = jnp.stack(
            split3(lse.transpose(0, 2, 1).reshape(jcount, 32))
            + split3(delta.transpose(0, 2, 1).reshape(jcount, 32))
        )
        payload = jnp.concatenate(
            [heads_first(queries), heads_first(grad_output), aux.reshape(-1, 128)], axis=0
        )
        pair = jnp.stack([key_states, value_states])

    with jax.named_scope("gather_kv_zh"):
        kv = jnp.stack(
            [pair] + [lax.ppermute(pair, "col", col_perm(0, -s, 0)) for s in range(1, NZH)]
        )
    with jax.named_scope("gather_q_zl"):
        got = [payload] + [
            lax.ppermute(payload, "row", row_perm(0, -s)) for s in range(1, NZL)
        ]
        wide = jnp.concatenate(
            [part[:rows] for part in got]
            + [part[rows : 2 * rows] for part in got]
            + [
                jnp.concatenate(
                    [part[2 * rows :].reshape(6, jcount, 32) for part in got], axis=2
                ).reshape(6 * jcount, 128)
            ],
            axis=0,
        )
    with jax.named_scope("gather_kv_y"):
        kv = jnp.stack(
            [kv] + [lax.ppermute(kv, "col", col_perm(-s, 0, 0)) for s in range(1, NY)]
        ).reshape(NY * NZH, 2, 128, 128)
    with jax.named_scope("gather_kv_core"):
        kv_other = lax.ppermute(kv, "col", col_perm(0, 0, 1))
    with jax.named_scope("gather_q_x"):
        pays = [wide] + [lax.ppermute(wide, "row", row_perm(-s, 0)) for s in range(1, NX)]

    table = segment_table(segment, prefix)
    *dqs, dkv = run_attention(
        ids, table, block_list[:, 0, 0, :], block_count[:, 0, 0], pays, kv, kv_other, jcount
    )

    with jax.named_scope("scatter_kv_core"):
        mine = total([dkv[0], lax.ppermute(dkv[1], "col", col_perm(0, 0, 1))])
        mine = mine.reshape(NY, NZH, 2, 128, 128)
    with jax.named_scope("scatter_q_x"):
        dq = total(
            [dqs[0]] + [lax.ppermute(dqs[s], "row", row_perm(s, 0)) for s in range(1, NX)]
        ).reshape(NZL, rows, 128)
    with jax.named_scope("scatter_kv_y"):
        mine = total(
            [mine[0]] + [lax.ppermute(mine[s], "col", col_perm(s, 0, 0)) for s in range(1, NY)]
        )
    with jax.named_scope("scatter_q_zl"):
        dq = total(
            [dq[0]] + [lax.ppermute(dq[s], "row", row_perm(0, s)) for s in range(1, NZL)]
        )
    with jax.named_scope("scatter_kv_zh"):
        mine = total(
            [mine[0]] + [lax.ppermute(mine[s], "col", col_perm(0, s, 0)) for s in range(1, NZH)]
        )
    dq = dq.reshape(jcount, 4, 8, 128).transpose(0, 2, 1, 3).reshape(jcount, 1, 8, 512)
    return dq, mine[0], mine[1]


def solution(mesh):
    in_specs = (
        P(None, "col", "row", None),
        P(None, "col", "row", None),
        P(None, "col", "row", None),
        P(("row", "col"), None),
        P(("row", "col"), None),
        P(None, "col", "row", None),
        P(),
        P(),
        P(None, "col", "row", None),
        P(None, "col", "row"),
    )
    out_specs = (P(None, "col", "row", None), P(("row", "col"), None), P(("row", "col"), None))
    return jax.shard_map(
        on_device, mesh=mesh, in_specs=in_specs, out_specs=out_specs, check_vma=False
    )
```

```python
import functools
import itertools

import jax
import jax.numpy as jnp
from jax import lax
from jax.experimental import pallas as pl
from jax.experimental.pallas import tpu as pltpu
from jax.sharding import PartitionSpec as P

NX, NZL, NY, NZH, NCORE = 4, 4, 4, 4, 2
SEGMENTS = 11
LOG2E = 1.4426950408889634
ROUND = 4


def flat(x, zl, y, zh, core):
    return (((x * NZL + zl) * NY + y) * NZH + zh) * NCORE + core


def spans(*sizes):
    return itertools.product(*(range(size) for size in sizes))


COLUMNS = [
    [flat(x, zl, y, zh, core) for y in range(NY)]
    for x, zl, zh, core in spans(NX, NZL, NZH, NCORE)
]
DEALS = [
    [flat((x - zh) % NX, (zl - zh) % NZL, y, zh, core) for zh in range(NZH)]
    for x, zl, y, core in spans(NX, NZL, NY, NCORE)
]


def exchange(value, members):
    return lax.all_to_all(value, ("row", "col"), 0, 0, axis_index_groups=members)


def gather(value, members):
    return exchange(jnp.broadcast_to(value, (4,) + value.shape), members)


def shift_x(value, by):
    pairs = [(x * NZL + zl, ((x + by) % NX) * NZL + zl) for x, zl in spans(NX, NZL)]
    return lax.ppermute(value, "row", pairs)


def flip_zl(value, bits):
    return lax.ppermute(value, "row", [(row, row ^ bits) for row in range(NX * NZL)])


def flip_core(value):
    return lax.ppermute(value, "col", [(col, col ^ 1) for col in range(NY * NZH * NCORE)])


def split3(value):
    high = lax.reduce_precision(value, 8, 7)
    rest = value - high
    mid = lax.reduce_precision(rest, 8, 7)
    low = rest - mid
    return [part.astype(jnp.bfloat16) for part in (high, mid, low)]


def segment_table(segment, prefix):
    ids = jnp.arange(SEGMENTS, dtype=jnp.int32)
    start = jnp.sum((segment[None, :] < ids[:, None]).astype(jnp.int32), axis=1)
    finish = jnp.sum((segment[None, :] <= ids[:, None]).astype(jnp.int32), axis=1)
    owner = jnp.max(jnp.where(segment[None, :] == ids[:, None], prefix[None, :], 0), axis=1)
    picked = owner[:, None] == ids[None, :]
    low = jnp.sum(jnp.where(picked, start[None, :], 0), axis=1)
    high = jnp.sum(jnp.where(picked, finish[None, :], 0), axis=1)
    return jnp.stack([start, low, high, finish])


def attention_kernel(jcount, ids_ref, table_ref, *refs):
    f32, bf16 = jnp.float32, jnp.bfloat16
    rows = jcount * 32
    own_ref, second_ref, outer_ref = refs[0:3]
    ahead_near, ahead_far, behind_near, behind_far, opposite_even, opposite_odd = refs[3:9]
    kv0, kv1 = refs[9:11]
    dqs, mine_ref, other_ref = refs[11:15], refs[15], refs[16]
    (
        k_scr,
        v_scr,
        kt_scr,
        dk_scr,
        dv_scr,
        lse_scr,
        delta_scr,
        q_scr,
        do_scr,
        qt_scr,
        dot_scr,
        dqt_scr,
        low_scr,
        pre_low_scr,
        pre_high_scr,
        place_scr,
        full_list,
        part_list,
    ) = refs[17:]
    scale = 128.0 ** -0.5
    my_x, my_zl, my_c = ids_ref[0], ids_ref[1], ids_ref[2]
    deal_x, deal_zl, my_core = ids_ref[3], ids_ref[4], ids_ref[5]

    def source(xs, zs):
        if xs == 2:
            return (opposite_odd if zs & 1 else opposite_even).at[zs >> 1]
        if xs == 0:
            return outer_ref.at[zs >> 1] if zs & 1 else (second_ref if zs else own_ref)
        near, far = (ahead_near, ahead_far) if xs == 1 else (behind_near, behind_far)
        return far.at[{2: 0, 1: 1, 3: 2}[zs]] if zs else near

    dk_scr[...] = jnp.zeros_like(dk_scr)
    dv_scr[...] = jnp.zeros_like(dv_scr)
    dqt_scr[...] = jnp.zeros_like(dqt_scr)

    def prepare(slot, _):
        for half, ref in enumerate((kv0, kv1)):
            at = pl.ds(pl.multiple_of((half ^ my_core) * 128, 128), 128)
            k_scr[slot, at, :] = ref[slot, 0]
            v_scr[slot, at, :] = ref[slot, 1]
        kt_scr[slot] = k_scr[slot].T
        return 0

    lax.fori_loop(0, 16, prepare, 0)

    lane_part = lax.broadcasted_iota(jnp.int32, (4, 128), 1) >> 5
    for xs in range(NX):
        lanes = pl.ds(xs * 128, 128)
        for b in range(4):
            lse = jnp.zeros((4, 128), f32)
            delta = jnp.zeros((4, 128), f32)
            for zs in range(NZL):
                aux = source(xs, zs)[pl.ds(2 * rows, 32), :].astype(f32)
                turn = ((zs - b) * 32) % 128
                here = lane_part == zs
                lse_part = aux[0:4] + aux[4:8] + aux[8:12]
                delta_part = aux[12:16] + aux[16:20] + aux[20:24]
                if turn:
                    lse_part = pltpu.roll(lse_part, turn, 1)
                    delta_part = pltpu.roll(delta_part, turn, 1)
                lse = jnp.where(here, lse_part, lse)
                delta = jnp.where(here, delta_part, delta)
            lse_scr[b, :, lanes] = lse * LOG2E
            delta_scr[b, :, lanes] = delta

    lane = lax.broadcasted_iota(jnp.int32, (jcount, 512), 1)
    row_of = ((my_x + (lane >> 7)) & 3) * 4 + (my_zl ^ ((lane >> 5) & 3))
    block = lax.broadcasted_iota(jnp.int32, (jcount, 512), 0) * 32 + my_c
    place = block * 128 + row_of * 8 + (lane & 7)
    own_low = jnp.zeros_like(place)
    pre_low = jnp.zeros_like(place)
    pre_high = jnp.zeros_like(place)
    for s in range(SEGMENTS):
        here = place >= table_ref[0, s]
        own_low = jnp.where(here, table_ref[0, s], own_low)
        pre_low = jnp.where(here, table_ref[1, s], pre_low)
        pre_high = jnp.where(here, table_ref[2, s], pre_high)
    place_scr[...] = place
    low_scr[...] = own_low
    pre_low_scr[...] = pre_low
    pre_high_scr[...] = jnp.minimum(pre_high, place + 1)
    key_iota = lax.broadcasted_iota(jnp.int32, (256, 512), 0)

    def group_of(zh):
        return ((deal_x - zh) & 3) * 4 + ((deal_zl - zh) & 3)

    def first_of(slot):
        return (group_of(slot & 3) * 16 + slot) * 256

    def sort_block(j, counts):
        base = (j * 32 + my_c) * 128
        first_low, last_low = jnp.int32(0), jnp.int32(0)
        hull_low, hull_high = jnp.int32(1 << 30), jnp.int32(0)
        for s in range(SEGMENTS):
            start, low, high = table_ref[0, s], table_ref[1, s], table_ref[2, s]
            finish = table_ref[3, s]
            first_low = jnp.where(base >= start, start, first_low)
            last_low = jnp.where(base + 127 >= start, start, last_low)
            meets = (start <= base + 127) & (finish > base) & (finish > start)
            hull_low = jnp.where(meets, jnp.minimum(hull_low, low), hull_low)
            hull_high = jnp.where(meets, jnp.maximum(hull_high, high), hull_high)
        hull_high = jnp.minimum(hull_high, base + 128)
        single = first_low == last_low
        tile_high = jnp.where(single, jnp.minimum(hull_high, base + 1), 0)

        def seek(zh, counts):
            def look(y, counts):
                fulls, parts = counts
                slot = y * 4 + zh
                first = first_of(slot)
                active = (first <= base + 127) & (first + 255 >= first_low)
                active = active | ((first < hull_high) & (first + 255 >= hull_low))
                full = (first >= last_low) & (first + 255 <= base)
                full = full | (single & (first >= hull_low) & (first + 256 <= tile_high))
                full_list[fulls] = j * 16 + slot
                part_list[parts] = j * 16 + slot
                return (
                    fulls + jnp.where(active & full, 1, 0),
                    parts + jnp.where(active & jnp.logical_not(full), 1, 0),
                )

            return lax.fori_loop(0, jnp.where(group_of(zh) <= j, 4, 0), look, counts)

        for xs in range(NX):
            for zs in range(NZL):
                at = (xs * NZL + zs) * 32
                ref = source(xs, zs)
                q_scr[j, pl.ds(at, 32), :] = ref[pl.ds(j * 32, 32), :]
                do_scr[j, pl.ds(at, 32), :] = ref[pl.ds(rows + j * 32, 32), :]
        qt_scr[j] = q_scr[j].T
        dot_scr[j] = do_scr[j].T
        return lax.fori_loop(0, 4, seek, counts)

    zero = jnp.int32(0)
    full_count, part_count = lax.fori_loop(0, jcount, sort_block, (zero, zero))

    def work(items, masked):
        items = [(item >> 4, item & 15) for item in items]
        scores = [
            jnp.dot(k_scr[slot], qt_scr[j], preferred_element_type=f32) for j, slot in items
        ]
        weight_grads = [
            jnp.dot(v_scr[slot], dot_scr[j], preferred_element_type=f32) for j, slot in items
        ]
        weights_b, score_grads_b = [], []
        for (j, slot), score, weight_grad in zip(items, scores, weight_grads):
            lse_row = lse_scr[j & 3, pl.ds(j >> 2, 1), :]
            delta_row = delta_scr[j & 3, pl.ds(j >> 2, 1), :]
            weights = jnp.exp2(score * (scale * LOG2E) - lse_row)
            if masked:
                key_at = key_iota + first_of(slot)
                row = pl.ds(j, 1)
                own = (key_at >= low_scr[row, :]) & (key_at <= place_scr[row, :])
                pre = (key_at >= pre_low_scr[row, :]) & (key_at < pre_high_scr[row, :])
                weights = jnp.where(own | pre, weights, 0.0)
            score_grad = weights * (weight_grad - delta_row)
            weights_b.append(weights.astype(bf16))
            score_grads_b.append(score_grad.astype(bf16))
        for (j, slot), weight, score_grad in zip(items, weights_b, score_grads_b):
            dv_scr[slot] += jnp.dot(weight, do_scr[j], preferred_element_type=f32)
            dk_scr[slot] += jnp.dot(score_grad, q_scr[j], preferred_element_type=f32)
            dqt_scr[j] += jnp.dot(kt_scr[slot], score_grad, preferred_element_type=f32)

    def sweep(items, count, masked):
        begin = zero
        for size in (ROUND, 1):
            turns = (count - begin) // size

            def turn(at, _, begin=begin, size=size):
                work([items[begin + at * size + u] for u in range(size)], masked)
                return 0

            lax.fori_loop(0, turns, turn, 0)
            begin = begin + turns * size

    sweep(full_list, full_count, False)
    sweep(part_list, part_count, True)

    def write_queries(j, _):
        dq = (dqt_scr[j] * scale).astype(bf16).T
        for xs in range(NX):
            for zs in range(NZL):
                at = (xs * NZL + zs) * 32
                dqs[xs][pl.ds(zs * rows + j * 32, 32), :] = dq[at : at + 32]
        return 0

    lax.fori_loop(0, jcount, write_queries, 0)

    def finish(slot, _):
        for half, ref in enumerate((mine_ref, other_ref)):
            at = pl.ds(pl.multiple_of((half ^ my_core) * 128, 128), 128)
            ref[slot, 0] = (dk_scr[slot, at, :] * scale).astype(bf16)
            ref[slot, 1] = dv_scr[slot, at, :].astype(bf16)
        return 0

    lax.fori_loop(0, 16, finish, 0)


def run_attention(ids, table, payloads, kv0, kv1, jcount):
    f32, bf16 = jnp.float32, jnp.bfloat16
    rows = jcount * 32
    smem = pl.BlockSpec(memory_space=pltpu.SMEM)
    vmem = pl.BlockSpec(memory_space=pltpu.VMEM)
    part = jax.ShapeDtypeStruct((NZL * rows, 128), bf16)
    return pl.pallas_call(
        functools.partial(attention_kernel, jcount),
        out_shape=[part] * 4 + [jax.ShapeDtypeStruct((16, 2, 128, 128), bf16)] * 2,
        in_specs=[smem] * 2 + [vmem] * 11,
        out_specs=[vmem] * 6,
        scratch_shapes=[
            pltpu.VMEM((16, 256, 128), bf16),
            pltpu.VMEM((16, 256, 128), bf16),
            pltpu.VMEM((16, 128, 256), bf16),
            pltpu.VMEM((16, 256, 128), f32),
            pltpu.VMEM((16, 256, 128), f32),
            pltpu.VMEM((4, 4, 512), f32),
            pltpu.VMEM((4, 4, 512), f32),
            pltpu.VMEM((jcount, 512, 128), bf16),
            pltpu.VMEM((jcount, 512, 128), bf16),
            pltpu.VMEM((jcount, 128, 512), bf16),
            pltpu.VMEM((jcount, 128, 512), bf16),
            pltpu.VMEM((jcount, 128, 512), f32),
            pltpu.VMEM((jcount, 512), jnp.int32),
            pltpu.VMEM((jcount, 512), jnp.int32),
            pltpu.VMEM((jcount, 512), jnp.int32),
            pltpu.VMEM((jcount, 512), jnp.int32),
            pltpu.SMEM((jcount * 16 + 1,), jnp.int32),
            pltpu.SMEM((jcount * 16 + 1,), jnp.int32),
        ],
        compiler_params=pltpu.CompilerParams(vmem_limit_bytes=48 * 1024 * 1024),
        name="attention_backward",
    )(ids, table, *payloads, kv0, kv1)


def total(parts):
    out = parts[0].astype(jnp.float32)
    for part in parts[1:]:
        out = out + part.astype(jnp.float32)
    return out.astype(jnp.bfloat16)


def on_device(
    queries,
    grad_output,
    attn_output,
    key_states,
    value_states,
    log_sum,
    segment,
    prefix,
    block_list,
    block_count,
):
    jcount = queries.shape[0]
    rows = jcount * 32
    row = lax.axis_index("row")
    col = lax.axis_index("col")
    my_x, my_zl, my_zh = row // NZL, row % NZL, (col // NCORE) % NZH
    ids = jnp.stack([my_x, my_zl, col, my_x + my_zh, my_zl + my_zh, col % NCORE])
    ids = ids.astype(jnp.int32)

    def heads_first(value):
        return value.reshape(jcount, 8, 4, 128).transpose(0, 2, 1, 3).reshape(rows, 128)

    with jax.named_scope("pack"):
        delta = jnp.sum(
            (grad_output.astype(jnp.float32) * attn_output.astype(jnp.float32)).reshape(
                jcount, 8, 4, 128
            ),
            axis=3,
        )
        lse = log_sum.reshape(jcount, 8, 4)
        aux = jnp.stack(
            split3(lse.transpose(0, 2, 1).reshape(jcount, 32))
            + split3(delta.transpose(0, 2, 1).reshape(jcount, 32))
        )
        payload = jnp.concatenate(
            [
                heads_first(queries),
                heads_first(grad_output),
                aux.reshape(-1, 128),
                jnp.zeros((8, 128), jnp.bfloat16),
            ],
            axis=0,
        )
        pair = jnp.stack([key_states, value_states])

    with jax.named_scope("gather_q_zl"):
        second = flip_zl(payload, 2)
        outer = flip_zl(jnp.stack([payload, second]), 1)
        others = jnp.concatenate([second[None], outer], axis=0)
    with jax.named_scope("gather_q_near"):
        near = [shift_x(payload, -1), shift_x(payload, 1)]
    with jax.named_scope("gather_kv_deal"):
        kv = gather(pair, DEALS)
    with jax.named_scope("gather_q_far"):
        others, *near = lax.optimization_barrier((others, *near))
        far = [shift_x(others, -1), shift_x(others, 1)]
    with jax.named_scope("gather_kv_y"):
        kv = gather(kv, COLUMNS).reshape(NY * NZH, 2, 128, 128)
    with jax.named_scope("gather_q_relay"):
        even = shift_x(jnp.stack([near[0], far[0][0]]), -1)
        odd = shift_x(far[1][1:], 1)
    with jax.named_scope("gather_kv_core"):
        kv_other = flip_core(kv)

    table = segment_table(segment, prefix)
    payloads = [payload, second, outer, near[0], far[0], near[1], far[1], even, odd]
    *dqs, mine, other = run_attention(ids, table, payloads, kv, kv_other, jcount)

    with jax.named_scope("scatter_kv_core"):
        mine = total([mine, flip_core(other)]).reshape(NY, NZH, 2, 128, 128)
    with jax.named_scope("scatter_q_relay"):
        even = shift_x(dqs[2][: 2 * rows], 1)
        odd = shift_x(dqs[2][2 * rows :], -1)
    with jax.named_scope("scatter_kv_y"):
        mine = total(exchange(mine, COLUMNS))
    with jax.named_scope("scatter_q_x"):
        ahead = total([dqs[1], jnp.concatenate([even, jnp.zeros_like(even)])])
        behind = total([dqs[3], jnp.concatenate([jnp.zeros_like(odd), odd])])
        dq = total([dqs[0], shift_x(ahead, 1), shift_x(behind, -1)])
    with jax.named_scope("scatter_kv_deal"):
        mine = total(exchange(mine, DEALS))
    with jax.named_scope("scatter_q_zl"):
        dq = dq.reshape(NZL, rows, 128)
        dq = total([dq[0::2], flip_zl(dq[1::2], 1)])
        dq = total([dq[0], flip_zl(dq[1], 2)])
    dq = dq.reshape(jcount, 4, 8, 128).transpose(0, 2, 1, 3).reshape(jcount, 1, 8, 512)
    return dq, mine[0], mine[1]


def solution(mesh):
    in_specs = (
        P(None, "col", "row", None),
        P(None, "col", "row", None),
        P(None, "col", "row", None),
        P(("row", "col"), None),
        P(("row", "col"), None),
        P(None, "col", "row", None),
        P(),
        P(),
        P(None, "col", "row", None),
        P(None, "col", "row"),
    )
    out_specs = (P(None, "col", "row", None), P(("row", "col"), None), P(("row", "col"), None))
    return jax.shard_map(
        on_device, mesh=mesh, in_specs=in_specs, out_specs=out_specs, check_vma=False
    )
```

```python
import functools
import itertools

import jax
import jax.numpy as jnp
from jax import lax
from jax.experimental import pallas as pl
from jax.experimental.pallas import tpu as pltpu
from jax.sharding import PartitionSpec as P

NX, NZL, NY, NZH, NCORE = 4, 4, 4, 4, 2
SEGMENTS = 11
LOG2E = 1.4426950408889634
ROUNDS = (4, 2, 1)


def flat(x, zl, y, zh, core):
    return (((x * NZL + zl) * NY + y) * NZH + zh) * NCORE + core


def spans(*sizes):
    return itertools.product(*(range(size) for size in sizes))


COLUMNS = [
    [flat(x, zl, y, zh, core) for y in range(NY)]
    for x, zl, zh, core in spans(NX, NZL, NZH, NCORE)
]
DEALS = [
    [flat((x - zh) % NX, (zl - zh) % NZL, y, zh, core) for zh in range(NZH)]
    for x, zl, y, core in spans(NX, NZL, NY, NCORE)
]


def exchange(value, members):
    return lax.all_to_all(value, ("row", "col"), 0, 0, axis_index_groups=members)


def gather(value, members):
    return exchange(jnp.broadcast_to(value, (4,) + value.shape), members)


def shift_x(value, by):
    pairs = [(x * NZL + zl, ((x + by) % NX) * NZL + zl) for x, zl in spans(NX, NZL)]
    return lax.ppermute(value, "row", pairs)


def flip_zl(value, bits):
    return lax.ppermute(value, "row", [(row, row ^ bits) for row in range(NX * NZL)])


def flip_deal(value, bits):
    pairs = []
    for x, zl, y, zh, core in spans(NX, NZL, NY, NZH, NCORE):
        back = (zh ^ bits) - zh
        there = flat((x - back) % NX, (zl - back) % NZL, y, zh ^ bits, core)
        pairs.append((flat(x, zl, y, zh, core), there))
    return lax.ppermute(value, ("row", "col"), pairs)


def flip_core(value):
    return lax.ppermute(value, "col", [(col, col ^ 1) for col in range(NY * NZH * NCORE)])


def split3(value):
    high = lax.reduce_precision(value, 8, 7)
    rest = value - high
    mid = lax.reduce_precision(rest, 8, 7)
    low = rest - mid
    return [part.astype(jnp.bfloat16) for part in (high, mid, low)]


def segment_table(segment, prefix):
    ids = jnp.arange(SEGMENTS, dtype=jnp.int32)
    start = jnp.sum((segment[None, :] < ids[:, None]).astype(jnp.int32), axis=1)
    finish = jnp.sum((segment[None, :] <= ids[:, None]).astype(jnp.int32), axis=1)
    owner = jnp.max(jnp.where(segment[None, :] == ids[:, None], prefix[None, :], 0), axis=1)
    picked = owner[:, None] == ids[None, :]
    low = jnp.sum(jnp.where(picked, start[None, :], 0), axis=1)
    high = jnp.sum(jnp.where(picked, finish[None, :], 0), axis=1)
    return jnp.stack([start, low, high, finish])


def list_kernel(jcount, ids_ref, table_ref, items_ref, count_ref):
    my_c, deal_x, deal_zl = ids_ref[2], ids_ref[3], ids_ref[4]
    firsts = []
    for slot in range(16):
        group = ((deal_x - slot) & 3) * 4 + ((deal_zl - slot) & 3)
        firsts.append((group * 16 + slot) * 256)

    def list_block(j, counts):
        base = (j * 32 + my_c) * 128
        first_low, last_low = jnp.int32(0), jnp.int32(0)
        hull_low, hull_high = jnp.int32(1 << 30), jnp.int32(0)
        for s in range(SEGMENTS):
            start, low, high = table_ref[0, s], table_ref[1, s], table_ref[2, s]
            finish = table_ref[3, s]
            first_low = jnp.where(base >= start, start, first_low)
            last_low = jnp.where(base + 127 >= start, start, last_low)
            meets = (start <= base + 127) & (finish > base) & (finish > start)
            hull_low = jnp.where(meets, jnp.minimum(hull_low, low), hull_low)
            hull_high = jnp.where(meets, jnp.maximum(hull_high, high), hull_high)
        hull_high = jnp.minimum(hull_high, base + 128)
        single = first_low == last_low
        tile_high = jnp.where(single, jnp.minimum(hull_high, base + 1), 0)
        fulls, parts = counts
        for slot, first in enumerate(firsts):
            own = (first <= base + 127) & (first + 255 >= first_low)
            active = own | ((first < hull_high) & (first + 255 >= hull_low))
            full = (first >= last_low) & (first + 255 <= base)
            full = full | ((first >= hull_low) & (first + 256 <= tile_high))
            items_ref[0, fulls] = j * 16 + slot
            items_ref[1, parts] = j * 16 + slot
            fulls = fulls + jnp.where(active & full, 1, 0)
            parts = parts + jnp.where(active & jnp.logical_not(full), 1, 0)
        return fulls, parts

    zero = jnp.int32(0)
    count_ref[0], count_ref[1] = lax.fori_loop(0, jcount, list_block, (zero, zero))


def list_items(ids, table, jcount):
    smem = pl.BlockSpec(memory_space=pltpu.SMEM)
    return pl.pallas_call(
        functools.partial(list_kernel, jcount),
        out_shape=[
            jax.ShapeDtypeStruct((2, jcount * 16 + 1), jnp.int32),
            jax.ShapeDtypeStruct((2,), jnp.int32),
        ],
        in_specs=[smem] * 2,
        out_specs=[smem] * 2,
        name="list_items",
    )(ids, table)


def attention_kernel(jcount, ids_ref, table_ref, items_ref, count_ref, *refs):
    f32, bf16 = jnp.float32, jnp.bfloat16
    rows = jcount * 32
    own_ref, second_ref, outer_ref = refs[0:3]
    ahead_near, ahead_far, behind_near, behind_far, opposite_even, opposite_odd = refs[3:9]
    kv0, kv1, mine_ref, other_ref = refs[9:11] + refs[15:17]
    dqs = refs[11:15]
    (
        k_scr,
        v_scr,
        kt_scr,
        dk_scr,
        dv_scr,
        lse_scr,
        delta_scr,
        q_scr,
        do_scr,
        qt_scr,
        dot_scr,
        dqt_scr,
        low_scr,
        pre_low_scr,
        pre_high_scr,
        place_scr,
    ) = refs[17:]
    scale = 128.0 ** -0.5
    my_x, my_zl, my_c = ids_ref[0], ids_ref[1], ids_ref[2]
    deal_x, deal_zl, my_core, my_zh = ids_ref[3], ids_ref[4], ids_ref[5], ids_ref[6]

    def source(xs, zs):
        if xs == 2:
            return (opposite_odd if zs & 1 else opposite_even).at[zs >> 1]
        if xs == 0:
            return outer_ref.at[zs >> 1] if zs & 1 else (second_ref if zs else own_ref)
        near, far = (ahead_near, ahead_far) if xs == 1 else (behind_near, behind_far)
        return far.at[{2: 0, 1: 1, 3: 2}[zs]] if zs else near

    dk_scr[...] = jnp.zeros_like(dk_scr)
    dv_scr[...] = jnp.zeros_like(dv_scr)
    dqt_scr[...] = jnp.zeros_like(dqt_scr)

    def prepare(slot, _):
        for half, ref in enumerate((kv0, kv1)):
            at = pl.ds(pl.multiple_of((half ^ my_core) * 128, 128), 128)
            k_scr[slot, at, :] = ref[slot, 0]
            v_scr[slot, at, :] = ref[slot, 1]
        kt_scr[slot] = k_scr[slot].T
        return 0

    lax.fori_loop(0, 16, prepare, 0)

    lane_part = lax.broadcasted_iota(jnp.int32, (4, 128), 1) >> 5
    for xs in range(NX):
        lanes = pl.ds(xs * 128, 128)
        pieces = []
        for zs in range(NZL):
            aux = source(xs, zs)[pl.ds(2 * rows, 32), :].astype(f32)
            pieces.append((aux[0:4] + aux[4:8] + aux[8:12], aux[12:16] + aux[16:20] + aux[20:24]))
        for b in range(4):
            lse = jnp.zeros((4, 128), f32)
            delta = jnp.zeros((4, 128), f32)
            for zs, (lse_part, delta_part) in enumerate(pieces):
                turn = ((zs - b) * 32) % 128
                here = lane_part == zs
                if turn:
                    lse_part = pltpu.roll(lse_part, turn, 1)
                    delta_part = pltpu.roll(delta_part, turn, 1)
                lse = jnp.where(here, lse_part, lse)
                delta = jnp.where(here, delta_part, delta)
            lse_scr[b, :, lanes] = lse * LOG2E
            delta_scr[b, :, lanes] = delta

    lane = lax.broadcasted_iota(jnp.int32, (jcount, 512), 1)
    row_of = ((my_x + (lane >> 7)) & 3) * 4 + (my_zl ^ ((lane >> 5) & 3))
    block = lax.broadcasted_iota(jnp.int32, (jcount, 512), 0) * 32 + my_c
    place = block * 128 + row_of * 8 + (lane & 7)
    own_low = jnp.zeros_like(place)
    pre_low = jnp.zeros_like(place)
    pre_high = jnp.zeros_like(place)
    for s in range(SEGMENTS):
        here = place >= table_ref[0, s]
        own_low = jnp.where(here, table_ref[0, s], own_low)
        pre_low = jnp.where(here, table_ref[1, s], pre_low)
        pre_high = jnp.where(here, table_ref[2, s], pre_high)
    place_scr[...] = place
    low_scr[...] = own_low
    pre_low_scr[...] = pre_low
    pre_high_scr[...] = jnp.minimum(pre_high, place + 1)
    key_iota = lax.broadcasted_iota(jnp.int32, (256, 512), 0)

    def group_of(zh):
        return ((deal_x - zh) & 3) * 4 + ((deal_zl - zh) & 3)

    def first_of(slot):
        return (group_of(slot & 3) * 16 + slot) * 256

    def take_block(j, _):
        for xs in range(NX):
            for zs in range(NZL):
                at = (xs * NZL + zs) * 32
                ref = source(xs, zs)
                q_scr[j, pl.ds(at, 32), :] = ref[pl.ds(j * 32, 32), :]
                do_scr[j, pl.ds(at, 32), :] = ref[pl.ds(rows + j * 32, 32), :]
        qt_scr[j] = q_scr[j].T
        dot_scr[j] = do_scr[j].T
        return 0

    lax.fori_loop(0, jcount, take_block, 0)

    def work(items, masked):
        items = [(item >> 4, item & 15) for item in items]
        scores = [
            jnp.dot(k_scr[slot], qt_scr[j], preferred_element_type=f32) for j, slot in items
        ]
        weight_grads = [
            jnp.dot(v_scr[slot], dot_scr[j], preferred_element_type=f32) for j, slot in items
        ]
        weights_b, score_grads_b = [], []
        for (j, slot), score, weight_grad in zip(items, scores, weight_grads):
            lse_row = lse_scr[j & 3, pl.ds(j >> 2, 1), :]
            delta_row = delta_scr[j & 3, pl.ds(j >> 2, 1), :]
            weights = jnp.exp2(score * (scale * LOG2E) - lse_row)
            if masked:
                key_at = key_iota + first_of(slot)
                row = pl.ds(j, 1)
                own = (key_at >= low_scr[row, :]) & (key_at <= place_scr[row, :])
                pre = (key_at >= pre_low_scr[row, :]) & (key_at < pre_high_scr[row, :])
                weights = jnp.where(own | pre, weights, 0.0)
            score_grad = weights * (weight_grad - delta_row)
            weights_b.append(weights.astype(bf16))
            score_grads_b.append(score_grad.astype(bf16))
        for (j, slot), weight, score_grad in zip(items, weights_b, score_grads_b):
            dv_scr[slot] += jnp.dot(weight, do_scr[j], preferred_element_type=f32)
            dk_scr[slot] += jnp.dot(score_grad, q_scr[j], preferred_element_type=f32)
            dqt_scr[j] += jnp.dot(kt_scr[slot], score_grad, preferred_element_type=f32)

    def sweep(kind, masked):
        count = count_ref[kind]
        begin = jnp.int32(0)
        for size in ROUNDS:
            turns = (count - begin) // size

            def turn(at, _, begin=begin, size=size):
                work([items_ref[kind, begin + at * size + u] for u in range(size)], masked)
                return 0

            lax.fori_loop(0, turns, turn, 0)
            begin = begin + turns * size

    sweep(0, False)
    sweep(1, True)

    def write_queries(j, _):
        dq = (dqt_scr[j] * scale).astype(bf16).T
        for xs in range(NX):
            for zs in range(NZL):
                at = (xs * NZL + zs) * 32
                dqs[xs][pl.ds(zs * rows + j * 32, 32), :] = dq[at : at + 32]
        return 0

    lax.fori_loop(0, jcount, write_queries, 0)

    def finish(slot, _):
        bits = (slot & 3) ^ my_zh
        out = (slot & 12) + jnp.where(bits == 3, 1, jnp.where(bits == 0, 0, bits + 1))
        for half, ref in enumerate((mine_ref, other_ref)):
            at = pl.ds(pl.multiple_of((half ^ my_core) * 128, 128), 128)
            ref[out, 0] = (dk_scr[slot, at, :] * scale).astype(bf16)
            ref[out, 1] = dv_scr[slot, at, :].astype(bf16)
        return 0

    lax.fori_loop(0, 16, finish, 0)


def run_attention(ids, table, items, counts, payloads, kv0, kv1, jcount):
    f32, bf16 = jnp.float32, jnp.bfloat16
    rows = jcount * 32
    smem = pl.BlockSpec(memory_space=pltpu.SMEM)
    vmem = pl.BlockSpec(memory_space=pltpu.VMEM)
    return pl.pallas_call(
        functools.partial(attention_kernel, jcount),
        out_shape=[jax.ShapeDtypeStruct((NZL * rows, 128), bf16)] * 4
        + [jax.ShapeDtypeStruct((16, 2, 128, 128), bf16)] * 2,
        in_specs=[smem] * 4 + [vmem] * 11,
        out_specs=[vmem] * 6,
        scratch_shapes=[
            pltpu.VMEM((16, 256, 128), bf16),
            pltpu.VMEM((16, 256, 128), bf16),
            pltpu.VMEM((16, 128, 256), bf16),
            pltpu.VMEM((16, 256, 128), f32),
            pltpu.VMEM((16, 256, 128), f32),
            pltpu.VMEM((4, 4, 512), f32),
            pltpu.VMEM((4, 4, 512), f32),
            pltpu.VMEM((jcount, 512, 128), bf16),
            pltpu.VMEM((jcount, 512, 128), bf16),
            pltpu.VMEM((jcount, 128, 512), bf16),
            pltpu.VMEM((jcount, 128, 512), bf16),
            pltpu.VMEM((jcount, 128, 512), f32),
            pltpu.VMEM((jcount, 512), jnp.int32),
            pltpu.VMEM((jcount, 512), jnp.int32),
            pltpu.VMEM((jcount, 512), jnp.int32),
            pltpu.VMEM((jcount, 512), jnp.int32),
        ],
        compiler_params=pltpu.CompilerParams(vmem_limit_bytes=48 * 1024 * 1024),
        name="attention_backward",
    )(ids, table, items, counts, *payloads, kv0, kv1)


def total(parts):
    out = parts[0].astype(jnp.float32)
    for part in parts[1:]:
        out = out + part.astype(jnp.float32)
    return out.astype(jnp.bfloat16)


def on_device(
    queries,
    grad_output,
    attn_output,
    key_states,
    value_states,
    log_sum,
    segment,
    prefix,
    block_list,
    block_count,
):
    jcount = queries.shape[0]
    rows = jcount * 32
    row = lax.axis_index("row")
    col = lax.axis_index("col")
    my_x, my_zl, my_zh = row // NZL, row % NZL, (col // NCORE) % NZH
    ids = jnp.stack([my_x, my_zl, col, my_x + my_zh, my_zl + my_zh, col % NCORE, my_zh])
    ids = ids.astype(jnp.int32)

    def heads_first(value):
        return value.reshape(jcount, 8, 4, 128).transpose(0, 2, 1, 3).reshape(rows, 128)

    with jax.named_scope("pack"):
        delta = jnp.sum(
            (grad_output.astype(jnp.float32) * attn_output.astype(jnp.float32)).reshape(
                jcount, 8, 4, 128
            ),
            axis=3,
        )
        lse = log_sum.reshape(jcount, 8, 4)
        aux = jnp.stack(
            split3(lse.transpose(0, 2, 1).reshape(jcount, 32))
            + split3(delta.transpose(0, 2, 1).reshape(jcount, 32))
        )
        payload = jnp.concatenate(
            [
                heads_first(queries),
                heads_first(grad_output),
                aux.reshape(-1, 128),
                jnp.zeros((8, 128), jnp.bfloat16),
            ],
            axis=0,
        )
        pair = jnp.stack([key_states, value_states])

    with jax.named_scope("gather_q_zl"):
        second = flip_zl(payload, 2)
        outer = flip_zl(jnp.stack([payload, second]), 1)
        others = jnp.concatenate([second[None], outer], axis=0)
    with jax.named_scope("gather_q_near"):
        payload, second = lax.optimization_barrier((payload, second))
        near = [shift_x(payload, -1), shift_x(payload, 1)]
    with jax.named_scope("gather_kv_deal"):
        kv = gather(pair, DEALS)
    with jax.named_scope("gather_q_far"):
        others, *near = lax.optimization_barrier((others, *near))
        far = [shift_x(others, -1), shift_x(others, 1)]
    with jax.named_scope("list_items"):
        table = segment_table(segment, prefix)
        items, counts = list_items(ids, table, jcount)
        kv, items, counts = lax.optimization_barrier((kv, items, counts))
    with jax.named_scope("gather_kv_y"):
        kv = gather(kv, COLUMNS).reshape(NY * NZH, 2, 128, 128)
    with jax.named_scope("gather_q_relay"):
        even = shift_x(jnp.stack([near[0], far[0][0]]), -1)
        odd = shift_x(far[1][1:], 1)
    with jax.named_scope("gather_kv_core"):
        kv_other = flip_core(kv)

    payloads = [payload, second, outer, near[0], far[0], near[1], far[1], even, odd]
    *dqs, mine, other = run_attention(ids, table, items, counts, payloads, kv, kv_other, jcount)

    with jax.named_scope("scatter_kv_core"):
        mine = total([mine, flip_core(other)]).reshape(NY, NZH, 2, 128, 128)
    with jax.named_scope("scatter_q_relay"):
        even = shift_x(dqs[2][: 2 * rows], 1)
        odd = shift_x(dqs[2][2 * rows :], -1)
    with jax.named_scope("scatter_kv_y"):
        mine = total(exchange(mine, COLUMNS))
    with jax.named_scope("scatter_q_x"):
        ahead = total([dqs[1], jnp.concatenate([even, jnp.zeros_like(even)])])
        behind = total([dqs[3], jnp.concatenate([jnp.zeros_like(odd), odd])])
        dq = total([dqs[0], shift_x(ahead, 1), shift_x(behind, -1)])
    with jax.named_scope("scatter_kv_deal"):
        mine = total([mine[:2], flip_deal(mine[2:], 1)])
        mine = total([mine[0], flip_deal(mine[1], 3)])
    with jax.named_scope("scatter_q_zl"):
        dq = dq.reshape(NZL, rows, 128)
        dq = total([dq[0::2], flip_zl(dq[1::2], 1)])
        dq = total([dq[0], flip_zl(dq[1], 2)])
    dq = dq.reshape(jcount, 4, 8, 128).transpose(0, 2, 1, 3).reshape(jcount, 1, 8, 512)
    return dq, mine[0], mine[1]


def solution(mesh):
    in_specs = (
        P(None, "col", "row", None),
        P(None, "col", "row", None),
        P(None, "col", "row", None),
        P(("row", "col"), None),
        P(("row", "col"), None),
        P(None, "col", "row", None),
        P(),
        P(),
        P(None, "col", "row", None),
        P(None, "col", "row"),
    )
    out_specs = (P(None, "col", "row", None), P(("row", "col"), None), P(("row", "col"), None))
    return jax.shard_map(
        on_device, mesh=mesh, in_specs=in_specs, out_specs=out_specs, check_vma=False
    )
```

```python
import functools
import itertools

import jax
import jax.numpy as jnp
from jax import lax
from jax.experimental import pallas as pl
from jax.experimental.pallas import tpu as pltpu
from jax.sharding import PartitionSpec as P

NX, NZL, NY, NZH, NCORE = 4, 4, 4, 4, 2
SEGMENTS = 11
LOG2E = 1.4426950408889634
ROUNDS = (4, 2, 1)


def flat(x, zl, y, zh, core):
    return (((x * NZL + zl) * NY + y) * NZH + zh) * NCORE + core


def spans(*sizes):
    return itertools.product(*(range(size) for size in sizes))


COLUMNS = [
    [flat(x, zl, y, zh, core) for y in range(NY)]
    for x, zl, zh, core in spans(NX, NZL, NZH, NCORE)
]
DEALS = [
    [flat((x - zh) % NX, (zl - zh) % NZL, y, zh, core) for zh in range(NZH)]
    for x, zl, y, core in spans(NX, NZL, NY, NCORE)
]


def exchange(value, members):
    return lax.all_to_all(value, ("row", "col"), 0, 0, axis_index_groups=members)


def gather(value, members):
    return exchange(jnp.broadcast_to(value, (4,) + value.shape), members)


def shift_x(value, by):
    pairs = [(x * NZL + zl, ((x + by) % NX) * NZL + zl) for x, zl in spans(NX, NZL)]
    return lax.ppermute(value, "row", pairs)


def flip_zl(value, bits):
    return lax.ppermute(value, "row", [(row, row ^ bits) for row in range(NX * NZL)])


def flip_core(value):
    return lax.ppermute(value, "col", [(col, col ^ 1) for col in range(NY * NZH * NCORE)])


def split3(value):
    high = lax.reduce_precision(value, 8, 7)
    rest = value - high
    mid = lax.reduce_precision(rest, 8, 7)
    low = rest - mid
    return [part.astype(jnp.bfloat16) for part in (high, mid, low)]


def segment_table(segment, prefix):
    ids = jnp.arange(SEGMENTS, dtype=jnp.int32)
    start = jnp.sum((segment[None, :] < ids[:, None]).astype(jnp.int32), axis=1)
    finish = jnp.sum((segment[None, :] <= ids[:, None]).astype(jnp.int32), axis=1)
    owner = jnp.max(jnp.where(segment[None, :] == ids[:, None], prefix[None, :], 0), axis=1)
    picked = owner[:, None] == ids[None, :]
    low = jnp.sum(jnp.where(picked, start[None, :], 0), axis=1)
    high = jnp.sum(jnp.where(picked, finish[None, :], 0), axis=1)
    return jnp.stack([start, low, high, finish])


def list_kernel(jcount, ids_ref, table_ref, items_ref, count_ref):
    my_c, deal_x, deal_zl = ids_ref[2], ids_ref[3], ids_ref[4]
    firsts = []
    for slot in range(16):
        group = ((deal_x - slot) & 3) * 4 + ((deal_zl - slot) & 3)
        firsts.append((group * 16 + slot) * 256)

    def list_block(j, counts):
        base = (j * 32 + my_c) * 128
        first_low, last_low = jnp.int32(0), jnp.int32(0)
        hull_low, hull_high = jnp.int32(1 << 30), jnp.int32(0)
        for s in range(SEGMENTS):
            start, low, high = table_ref[0, s], table_ref[1, s], table_ref[2, s]
            finish = table_ref[3, s]
            first_low = jnp.where(base >= start, start, first_low)
            last_low = jnp.where(base + 127 >= start, start, last_low)
            meets = (start <= base + 127) & (finish > base) & (finish > start)
            hull_low = jnp.where(meets, jnp.minimum(hull_low, low), hull_low)
            hull_high = jnp.where(meets, jnp.maximum(hull_high, high), hull_high)
        hull_high = jnp.minimum(hull_high, base + 128)
        single = first_low == last_low
        tile_high = jnp.where(single, jnp.minimum(hull_high, base + 1), 0)
        fulls, parts = counts
        for slot, first in enumerate(firsts):
            own = (first <= base + 127) & (first + 255 >= first_low)
            active = own | ((first < hull_high) & (first + 255 >= hull_low))
            full = (first >= last_low) & (first + 255 <= base)
            full = full | ((first >= hull_low) & (first + 256 <= tile_high))
            items_ref[0, fulls] = j * 16 + slot
            items_ref[1, parts] = j * 16 + slot
            fulls = fulls + jnp.where(active & full, 1, 0)
            parts = parts + jnp.where(active & jnp.logical_not(full), 1, 0)
        return fulls, parts

    zero = jnp.int32(0)
    count_ref[0], count_ref[1] = lax.fori_loop(0, jcount, list_block, (zero, zero))


def list_items(ids, table, jcount):
    smem = pl.BlockSpec(memory_space=pltpu.SMEM)
    return pl.pallas_call(
        functools.partial(list_kernel, jcount),
        out_shape=[
            jax.ShapeDtypeStruct((2, jcount * 16 + 1), jnp.int32),
            jax.ShapeDtypeStruct((2,), jnp.int32),
        ],
        in_specs=[smem] * 2,
        out_specs=[smem] * 2,
        name="list_items",
    )(ids, table)


def attention_kernel(jcount, ids_ref, table_ref, items_ref, count_ref, *refs):
    f32, bf16 = jnp.float32, jnp.bfloat16
    rows = jcount * 32
    own_ref, second_ref, outer_ref = refs[0:3]
    ahead_near, ahead_far, behind_near, behind_far, opposite_even, opposite_odd = refs[3:9]
    kv0, kv1, mine_ref, other_ref = refs[9:11] + refs[15:17]
    dqs = refs[11:15]
    (
        k_scr,
        v_scr,
        kt_scr,
        dk_scr,
        dv_scr,
        lse_scr,
        delta_scr,
        q_scr,
        do_scr,
        qt_scr,
        dot_scr,
        dqt_scr,
        low_scr,
        pre_low_scr,
        pre_high_scr,
        place_scr,
    ) = refs[17:]
    scale = 128.0 ** -0.5
    my_x, my_zl, my_c = ids_ref[0], ids_ref[1], ids_ref[2]
    deal_x, deal_zl, my_core = ids_ref[3], ids_ref[4], ids_ref[5]

    def source(xs, zs):
        if xs == 2:
            return (opposite_odd if zs & 1 else opposite_even).at[zs >> 1]
        if xs == 0:
            return outer_ref.at[zs >> 1] if zs & 1 else (second_ref if zs else own_ref)
        near, far = (ahead_near, ahead_far) if xs == 1 else (behind_near, behind_far)
        return far.at[{2: 0, 1: 1, 3: 2}[zs]] if zs else near

    dk_scr[...] = jnp.zeros_like(dk_scr)
    dv_scr[...] = jnp.zeros_like(dv_scr)
    dqt_scr[...] = jnp.zeros_like(dqt_scr)

    def prepare(slot, _):
        for half, ref in enumerate((kv0, kv1)):
            at = pl.ds(pl.multiple_of((half ^ my_core) * 128, 128), 128)
            k_scr[slot, at, :] = ref[slot, 0]
            v_scr[slot, at, :] = ref[slot, 1]
        kt_scr[slot] = k_scr[slot].T
        return 0

    lax.fori_loop(0, 16, prepare, 0)

    lane_part = lax.broadcasted_iota(jnp.int32, (4, 128), 1) >> 5
    for xs in range(NX):
        lanes = pl.ds(xs * 128, 128)
        pieces = []
        for zs in range(NZL):
            aux = source(xs, zs)[pl.ds(2 * rows, 32), :].astype(f32)
            pieces.append((aux[0:4] + aux[4:8] + aux[8:12], aux[12:16] + aux[16:20] + aux[20:24]))
        for b in range(4):
            lse = jnp.zeros((4, 128), f32)
            delta = jnp.zeros((4, 128), f32)
            for zs, (lse_part, delta_part) in enumerate(pieces):
                turn = ((zs - b) * 32) % 128
                here = lane_part == zs
                if turn:
                    lse_part = pltpu.roll(lse_part, turn, 1)
                    delta_part = pltpu.roll(delta_part, turn, 1)
                lse = jnp.where(here, lse_part, lse)
                delta = jnp.where(here, delta_part, delta)
            lse_scr[b, :, lanes] = lse * LOG2E
            delta_scr[b, :, lanes] = delta

    lane = lax.broadcasted_iota(jnp.int32, (jcount, 512), 1)
    row_of = ((my_x + (lane >> 7)) & 3) * 4 + (my_zl ^ ((lane >> 5) & 3))
    block = lax.broadcasted_iota(jnp.int32, (jcount, 512), 0) * 32 + my_c
    place = block * 128 + row_of * 8 + (lane & 7)
    own_low = jnp.zeros_like(place)
    pre_low = jnp.zeros_like(place)
    pre_high = jnp.zeros_like(place)
    for s in range(SEGMENTS):
        here = place >= table_ref[0, s]
        own_low = jnp.where(here, table_ref[0, s], own_low)
        pre_low = jnp.where(here, table_ref[1, s], pre_low)
        pre_high = jnp.where(here, table_ref[2, s], pre_high)
    place_scr[...] = place
    low_scr[...] = own_low
    pre_low_scr[...] = pre_low
    pre_high_scr[...] = jnp.minimum(pre_high, place + 1)
    key_iota = lax.broadcasted_iota(jnp.int32, (256, 512), 0)

    def group_of(zh):
        return ((deal_x - zh) & 3) * 4 + ((deal_zl - zh) & 3)

    def first_of(slot):
        return (group_of(slot & 3) * 16 + slot) * 256

    def take_block(j, _):
        for xs in range(NX):
            for zs in range(NZL):
                at = (xs * NZL + zs) * 32
                ref = source(xs, zs)
                q_scr[j, pl.ds(at, 32), :] = ref[pl.ds(j * 32, 32), :]
                do_scr[j, pl.ds(at, 32), :] = ref[pl.ds(rows + j * 32, 32), :]
        qt_scr[j] = q_scr[j].T
        dot_scr[j] = do_scr[j].T
        return 0

    lax.fori_loop(0, jcount, take_block, 0)

    def work(items, masked):
        items = [(item >> 4, item & 15) for item in items]
        scores = [
            jnp.dot(k_scr[slot], qt_scr[j], preferred_element_type=f32) for j, slot in items
        ]
        weight_grads = [
            jnp.dot(v_scr[slot], dot_scr[j], preferred_element_type=f32) for j, slot in items
        ]
        weights_b, score_grads_b = [], []
        for (j, slot), score, weight_grad in zip(items, scores, weight_grads):
            lse_row = lse_scr[j & 3, pl.ds(j >> 2, 1), :]
            delta_row = delta_scr[j & 3, pl.ds(j >> 2, 1), :]
            weights = jnp.exp2(score * (scale * LOG2E) - lse_row)
            if masked:
                key_at = key_iota + first_of(slot)
                row = pl.ds(j, 1)
                own = (key_at >= low_scr[row, :]) & (key_at <= place_scr[row, :])
                pre = (key_at >= pre_low_scr[row, :]) & (key_at < pre_high_scr[row, :])
                weights = jnp.where(own | pre, weights, 0.0)
            score_grad = weights * (weight_grad - delta_row)
            weights_b.append(weights.astype(bf16))
            score_grads_b.append(score_grad.astype(bf16))
        for (j, slot), weight, score_grad in zip(items, weights_b, score_grads_b):
            dv_scr[slot] += jnp.dot(weight, do_scr[j], preferred_element_type=f32)
            dk_scr[slot] += jnp.dot(score_grad, q_scr[j], preferred_element_type=f32)
            dqt_scr[j] += jnp.dot(kt_scr[slot], score_grad, preferred_element_type=f32)

    def sweep(kind, masked):
        count = count_ref[kind]
        begin = jnp.int32(0)
        for size in ROUNDS:
            turns = (count - begin) // size

            def turn(at, _, begin=begin, size=size):
                work([items_ref[kind, begin + at * size + u] for u in range(size)], masked)
                return 0

            lax.fori_loop(0, turns, turn, 0)
            begin = begin + turns * size

    sweep(0, False)
    sweep(1, True)

    def write_queries(j, _):
        dq = (dqt_scr[j] * scale).astype(bf16).T
        for xs in range(NX):
            for zs in range(NZL):
                at = (xs * NZL + zs) * 32
                dqs[xs][pl.ds(zs * rows + j * 32, 32), :] = dq[at : at + 32]
        return 0

    lax.fori_loop(0, jcount, write_queries, 0)

    def finish(slot, _):
        for half, ref in enumerate((mine_ref, other_ref)):
            at = pl.ds(pl.multiple_of((half ^ my_core) * 128, 128), 128)
            ref[slot, 0] = (dk_scr[slot, at, :] * scale).astype(bf16)
            ref[slot, 1] = dv_scr[slot, at, :].astype(bf16)
        return 0

    lax.fori_loop(0, 16, finish, 0)


def run_attention(ids, table, items, counts, payloads, kv0, kv1, jcount):
    f32, bf16 = jnp.float32, jnp.bfloat16
    rows = jcount * 32
    smem = pl.BlockSpec(memory_space=pltpu.SMEM)
    vmem = pl.BlockSpec(memory_space=pltpu.VMEM)
    return pl.pallas_call(
        functools.partial(attention_kernel, jcount),
        out_shape=[jax.ShapeDtypeStruct((NZL * rows, 128), bf16)] * 4
        + [jax.ShapeDtypeStruct((16, 2, 128, 128), bf16)] * 2,
        in_specs=[smem] * 4 + [vmem] * 11,
        out_specs=[vmem] * 6,
        scratch_shapes=[
            pltpu.VMEM((16, 256, 128), bf16),
            pltpu.VMEM((16, 256, 128), bf16),
            pltpu.VMEM((16, 128, 256), bf16),
            pltpu.VMEM((16, 256, 128), f32),
            pltpu.VMEM((16, 256, 128), f32),
            pltpu.VMEM((4, 4, 512), f32),
            pltpu.VMEM((4, 4, 512), f32),
            pltpu.VMEM((jcount, 512, 128), bf16),
            pltpu.VMEM((jcount, 512, 128), bf16),
            pltpu.VMEM((jcount, 128, 512), bf16),
            pltpu.VMEM((jcount, 128, 512), bf16),
            pltpu.VMEM((jcount, 128, 512), f32),
            pltpu.VMEM((jcount, 512), jnp.int32),
            pltpu.VMEM((jcount, 512), jnp.int32),
            pltpu.VMEM((jcount, 512), jnp.int32),
            pltpu.VMEM((jcount, 512), jnp.int32),
        ],
        compiler_params=pltpu.CompilerParams(vmem_limit_bytes=48 * 1024 * 1024),
        name="attention_backward",
    )(ids, table, items, counts, *payloads, kv0, kv1)


def total(parts):
    out = parts[0].astype(jnp.float32)
    for part in parts[1:]:
        out = out + part.astype(jnp.float32)
    return out.astype(jnp.bfloat16)


def on_device(
    queries,
    grad_output,
    attn_output,
    key_states,
    value_states,
    log_sum,
    segment,
    prefix,
    block_list,
    block_count,
):
    jcount = queries.shape[0]
    rows = jcount * 32
    row = lax.axis_index("row")
    col = lax.axis_index("col")
    my_x, my_zl, my_zh = row // NZL, row % NZL, (col // NCORE) % NZH
    ids = jnp.stack([my_x, my_zl, col, my_x + my_zh, my_zl + my_zh, col % NCORE])
    ids = ids.astype(jnp.int32)

    def heads_first(value):
        return value.reshape(jcount, 8, 4, 128).transpose(0, 2, 1, 3).reshape(rows, 128)

    with jax.named_scope("pack"):
        delta = jnp.sum(
            (grad_output.astype(jnp.float32) * attn_output.astype(jnp.float32)).reshape(
                jcount, 8, 4, 128
            ),
            axis=3,
        )
        lse = log_sum.reshape(jcount, 8, 4)
        aux = jnp.stack(
            split3(lse.transpose(0, 2, 1).reshape(jcount, 32))
            + split3(delta.transpose(0, 2, 1).reshape(jcount, 32))
        )
        payload = jnp.concatenate(
            [
                heads_first(queries),
                heads_first(grad_output),
                aux.reshape(-1, 128),
                jnp.zeros((8, 128), jnp.bfloat16),
            ],
            axis=0,
        )
        pair = jnp.stack([key_states, value_states])

    with jax.named_scope("gather_q_zl"):
        second = flip_zl(payload, 2)
        outer = flip_zl(jnp.stack([payload, second]), 1)
        others = jnp.concatenate([second[None], outer], axis=0)
    with jax.named_scope("gather_q_near"):
        payload, second = lax.optimization_barrier((payload, second))
        near = [shift_x(payload, -1), shift_x(payload, 1)]
    with jax.named_scope("gather_kv_deal"):
        kv = gather(pair, DEALS)
    with jax.named_scope("gather_q_far"):
        others, *near = lax.optimization_barrier((others, *near))
        far = [shift_x(others, -1), shift_x(others, 1)]
    with jax.named_scope("list_items"):
        table = segment_table(segment, prefix)
        items, counts = list_items(ids, table, jcount)
        kv, items, counts = lax.optimization_barrier((kv, items, counts))
    with jax.named_scope("gather_kv_y"):
        kv = gather(kv, COLUMNS).reshape(NY * NZH, 2, 128, 128)
    with jax.named_scope("gather_q_relay"):
        even = shift_x(jnp.stack([near[0], far[0][0]]), -1)
        odd = shift_x(far[1][1:], 1)
    with jax.named_scope("gather_kv_core"):
        kv_other = flip_core(kv)

    payloads = [payload, second, outer, near[0], far[0], near[1], far[1], even, odd]
    *dqs, mine, other = run_attention(ids, table, items, counts, payloads, kv, kv_other, jcount)

    with jax.named_scope("scatter_kv_core"):
        mine = total([mine, flip_core(other)]).reshape(NY, NZH, 2, 128, 128)
    with jax.named_scope("scatter_q_relay"):
        even = shift_x(dqs[2][: 2 * rows], 1)
        odd = shift_x(dqs[2][2 * rows :], -1)
    with jax.named_scope("scatter_kv_y"):
        mine = total(exchange(mine, COLUMNS))
    with jax.named_scope("scatter_q_x"):
        ahead = total([dqs[1], jnp.concatenate([even, jnp.zeros_like(even)])])
        behind = total([dqs[3], jnp.concatenate([jnp.zeros_like(odd), odd])])
        dq = total([dqs[0], shift_x(ahead, 1), shift_x(behind, -1)])
    with jax.named_scope("scatter_kv_deal"):
        mine = total(exchange(mine, DEALS))
    with jax.named_scope("scatter_q_zl"):
        dq = dq.reshape(NZL, rows, 128)
        dq = total([dq[0::2], flip_zl(dq[1::2], 1)])
        dq = total([dq[0], flip_zl(dq[1], 2)])
    dq = dq.reshape(jcount, 4, 8, 128).transpose(0, 2, 1, 3).reshape(jcount, 1, 8, 512)
    return dq, mine[0], mine[1]


def solution(mesh):
    in_specs = (
        P(None, "col", "row", None),
        P(None, "col", "row", None),
        P(None, "col", "row", None),
        P(("row", "col"), None),
        P(("row", "col"), None),
        P(None, "col", "row", None),
        P(),
        P(),
        P(None, "col", "row", None),
        P(None, "col", "row"),
    )
    out_specs = (P(None, "col", "row", None), P(("row", "col"), None), P(("row", "col"), None))
    return jax.shard_map(
        on_device, mesh=mesh, in_specs=in_specs, out_specs=out_specs, check_vma=False
    )
```
